32 devices in a mesh: grp: 4 (over z), dev: 8 (over y, x, core).
Axes of the slice: x: 2, y: 2, z: 4, core: 2. Of those that a mesh axis runs over, the one named last changes fastest.
Arguments:
- adjoint: bfloat16 [16384, 384], P(('grp', 'dev')), may hold values from -6 to 6
- state: bfloat16 [16384, 384], P(('grp', 'dev')), may hold values from -6 to 6
- interp: bfloat16 [64, 64], replicated, may hold values from -0.75 to 0.75
- flux_weights: float32 [3, 6, 6], replicated, may hold values from -2.5 to 2.5
- metric: float32 [16384, 64], P(('grp', 'dev')), may hold values from 0.3 to 3
- geometry: float32 [3, 64, 64], replicated, may hold values from -0.375 to 0.375
- connectivity: int32 [16384, 64], P(('grp', 'dev')), may hold values from 0 to 8415
- halo_source: int32 [256, 64], P(('grp', 'dev')), may hold values from 0 to 224, as said below
- halo_target: int32 [256, 64], P(('grp', 'dev')), may hold values from 0 to 8191
- surface_node: int32 [4096], P(('grp', 'dev')), may hold values from 0 to 8191
- surface_point: int32 [4096], P(('grp', 'dev')), may hold values from 0 to 39999
- point_coords: float32 [3, 40000], replicated, may hold values from 0 to 1
Outputs:
- node_partials: float32 [3, 262144], P(None, ('grp', 'dev'))
- point_gradient: float32 [3, 40000], P(None, 'grp')
The draws below stay inside these ranges and needn't reach their ends.
Inputs may be any that keep to these rules, and one draw needn't show every extreme that they name: `halo_source`: on each device, the row of the device itself holds only 224; every halo copy 0 to 223 stands in exactly one slot of the other rows; all other slots hold 224.
All inputs are finite; a program needn't handle non-finite values.
Results may differ from the reference program's by a relative error of at most 0.0003.
Values sent between devices are 32-bit elements; how exact they have to be, the bound alone decides.
No kernel may reach another device: no remote copies, remote signals or barrier semaphores. Data moves between devices by JAX's collectives and lax.ppermute only.
A program may use at most 768 MiB of HBM per device.

```python
import math
import jax
import jax.numpy as jnp
from jax import lax

V = 6
P_SIZE = 64
Q = 64
NN = 64
NCP = 40000
ITERS = 2
E_DEV = 512
SN = 128
HMAX = 64
NOWN = 8192
NHALO = 224
ELEMS = 16384
SURF = 4096
PEERS = 256
N_GRP = 4
N_DEV = 8


def draw_halo_source(key, part):
    key = jax.random.fold_in(key, 11)
    devices_all = N_GRP * N_DEV
    slot_total = (N_DEV - 1) * HMAX
    slot_values = jnp.minimum(jnp.arange(slot_total, dtype=jnp.int32), NHALO)
    device_keys = jax.random.split(key, devices_all)
    shuffled = jax.vmap(lambda subkey: jax.random.permutation(subkey, slot_values))(device_keys)
    shuffled = shuffled.reshape(devices_all, N_DEV - 1, HMAX)
    own_row = jnp.arange(devices_all, dtype=jnp.int32) % N_DEV
    row_ids = jnp.arange(N_DEV, dtype=jnp.int32)
    source_row = row_ids[None, :] - (row_ids[None, :] > own_row[:, None]).astype(jnp.int32)
    source_row = jnp.clip(source_row, 0, N_DEV - 2)
    source_full = jnp.broadcast_to(source_row[:, :, None], (devices_all, N_DEV, HMAX))
    picked = jnp.take_along_axis(shuffled, source_full, axis=1)
    result = jnp.where((row_ids[None, :] == own_row[:, None])[:, :, None], NHALO, picked)
    return result.reshape(devices_all * N_DEV, HMAX).astype(jnp.int32)


def with_ends(entries, stream_key, smallest, high):
    longest = entries.shape.index(max(entries.shape))
    spots = []
    for shift in (0, 1):
        where = [jax.random.randint(jax.random.fold_in(stream_key, axis), (), 0, length) for axis, length in enumerate(entries.shape)]
        where[longest] = (where[longest] + shift) % entries.shape[longest]
        spots.append(tuple(where))
    return entries.at[spots[0]].set(smallest).at[spots[1]].set(high)


def levels(own_key, dims, cuts, least, high):
    gain, own = 1.0, jax.random.fold_in(own_key, 6)
    for axis_at, parts in cuts:
        draws = jnp.exp(jax.random.uniform(jax.random.fold_in(own, axis_at), (parts,), jnp.float32, least / len(cuts), high / len(cuts)))
        gain = gain * jnp.repeat(draws, dims[axis_at] // parts).reshape([-1 if axis == axis_at else 1 for axis in range(len(dims))])
    return gain


def centred(stream_key, dims, spread, bound, cuts=(), kind=jnp.bfloat16):
    gain = levels(stream_key, dims, cuts, -0.22, 0.18) if cuts else 1.0
    values = jax.random.normal(stream_key, dims, jnp.float32) * spread * gain
    return jnp.minimum(jnp.maximum(values, -bound), bound).astype(kind)


def setup_inputs(seed: int = 0) -> dict:
    key_of = jax.random.split(jax.random.key(seed), 13)
    return {
        "adjoint": centred(key_of[0], (ELEMS, V * P_SIZE), 1.0, 6.0, ((0, 32),)),
        "state": centred(key_of[1], (ELEMS, V * P_SIZE), 1.0, 6.0, ((0, 32),)),
        "interp": centred(key_of[2], (P_SIZE, Q), P_SIZE ** -0.5, 0.75),
        "flux_weights": centred(key_of[3], (3, V, V), V ** -0.5, 2.5, (), jnp.float32),
        "metric": jnp.clip(jnp.exp(math.log(3.0) - 2.3025851 * jax.random.uniform(key_of[4], (ELEMS, Q), jnp.float32) ** levels(key_of[4], (ELEMS, Q), ((0, 32),), -0.2, 0.2)), 0.3, 3.0),
        "geometry": centred(key_of[5], (3, Q, NN), (4 * Q) ** -0.5, 0.375, (), jnp.float32),
        "connectivity": with_ends(jax.random.randint(key_of[6], (ELEMS, NN), 0, NOWN + NHALO), jax.random.fold_in(key_of[6], 1), 0, (NOWN + NHALO) - 1).astype(jnp.int32),
        "halo_source": draw_halo_source(jax.random.fold_in(key_of[12], 71), 0),
        "halo_target": with_ends(jax.random.randint(key_of[8], (PEERS, HMAX), 0, NOWN), jax.random.fold_in(key_of[8], 1), 0, NOWN - 1).astype(jnp.int32),
        "surface_node": with_ends(jax.random.randint(key_of[9], (SURF,), 0, NOWN), jax.random.fold_in(key_of[9], 1), 0, NOWN - 1).astype(jnp.int32),
        "surface_point": with_ends(jax.random.randint(key_of[10], (SURF,), 0, NCP), jax.random.fold_in(key_of[10], 1), 0, NCP - 1).astype(jnp.int32),
        "point_coords": jnp.clip(jax.random.uniform(key_of[11], (3, NCP), jnp.float32, 0.0, 1.0), 0.0, 1.0),
    }


ridge_weight = 4.0

def support_radius():
    return (168.0 / (4.18879 * NCP)) ** (1.0 / 3.0)

def wendland(row_coords, col_coords):
    dist_squared = jnp.zeros((row_coords.shape[1], col_coords.shape[1]), jnp.float32)
    for axis_number in range(3):
        differ = row_coords[axis_number][:, None] - col_coords[axis_number][None, :]
        dist_squared = dist_squared + differ * differ
    scaled = jnp.sqrt(dist_squared) / support_radius()
    remaining = jnp.maximum(1.0 - scaled, 0.0)
    return remaining ** 4 * (4.0 * scaled + 1.0)

def element_partials(adjoint_rows, state_rows, metric_rows, connectivity_rows, interp, flux_weights, geometry):
    elements = adjoint_rows.shape[0]
    basis_count = interp.shape[0]
    quad_points = interp.shape[1]
    variables = adjoint_rows.shape[1] // basis_count
    elem_nodes = geometry.shape[2]
    adjoint_quad = jnp.dot(adjoint_rows.reshape(elements * variables, basis_count), interp, preferred_element_type=jnp.float32).reshape(elements, variables, quad_points)
    state_quad = jnp.dot(state_rows.reshape(elements * variables, basis_count), interp, preferred_element_type=jnp.float32).reshape(elements, variables, quad_points)
    coupled = jnp.einsum('cvw,ewq->ecvq', flux_weights, state_quad, precision=lax.Precision.HIGHEST)
    weighted = lax.optimization_barrier(jnp.sum(adjoint_quad[:, None] * coupled, axis=2)) * metric_rows[:, None, :]
    partials = jnp.einsum('ecq,cqn->ecn', weighted, geometry, precision=lax.Precision.HIGHEST)
    nodal_sums = jax.ops.segment_sum(partials.transpose(0, 2, 1).reshape(elements * elem_nodes, 3), connectivity_rows.reshape(-1), num_segments=NOWN + NHALO)
    return nodal_sums.T

def take_columns(values, slot_index):
    return values[:, slot_index]

def sum_slots(values, slot_index):
    return jax.ops.segment_sum(values, slot_index, num_segments=NOWN)

def reference(adjoint, state, interp, flux_weights, metric, geometry, connectivity, halo_source, halo_target, surface_node, surface_point, point_coords):
    devices = N_GRP * N_DEV

    def per_device(items):
        return element_partials(items[0], items[1], items[2], items[3], interp, flux_weights, geometry)
    nodal_all = lax.map(per_device, (adjoint.reshape(devices, E_DEV, V * P_SIZE), state.reshape(devices, E_DEV, V * P_SIZE), metric.reshape(devices, E_DEV, Q), connectivity.reshape(devices, E_DEV, NN)))
    halo_values = jnp.concatenate([nodal_all[:, :, NOWN:], jnp.zeros((devices, 3, 1), jnp.float32)], axis=2)
    outgoing = jax.vmap(take_columns)(halo_values, halo_source.reshape(devices, N_DEV, HMAX))
    incoming = outgoing.reshape(N_GRP, N_DEV, 3, N_DEV, HMAX).transpose(0, 3, 1, 4, 2).reshape(devices, N_DEV * HMAX, 3)
    added = jax.vmap(sum_slots)(incoming, halo_target.reshape(devices, N_DEV * HMAX))
    owned = nodal_all[:, :, :NOWN] + added.transpose(0, 2, 1)
    node_partials = owned.transpose(1, 0, 2).reshape(3, devices * NOWN)
    surface_values = jax.vmap(take_columns)(owned, surface_node.reshape(devices, SN))
    right_side = jax.ops.segment_sum(surface_values.transpose(0, 2, 1).reshape(devices * SN, 3), surface_point, num_segments=NCP).T
    row_parts = point_coords.reshape(3, N_DEV, NCP // N_DEV).transpose(1, 0, 2)

    def apply_matrix(direction):

        def block_image(row_coords):
            return jnp.dot(wendland(row_coords, point_coords), direction.T, precision=lax.Precision.HIGHEST)
        blocks = lax.map(block_image, row_parts)
        return blocks.reshape(NCP, 3).T + ridge_weight * direction
    solution = jnp.zeros((3, NCP), jnp.float32)
    residual = right_side
    direction = right_side
    norm_now = lax.optimization_barrier(jnp.sum(residual * residual, axis=1))
    for iteration in range(ITERS):
        image = apply_matrix(direction)
        step_size = norm_now / lax.optimization_barrier(jnp.sum(direction * image, axis=1))
        solution = solution + step_size[:, None] * direction
        residual = residual - step_size[:, None] * image
        norm_next = lax.optimization_barrier(jnp.sum(residual * residual, axis=1))
        direction = residual + (norm_next / norm_now)[:, None] * direction
        norm_now = norm_next
    return (node_partials, solution)
```

```python
import functools

import jax
import jax.numpy as jnp
from jax import lax
from jax.experimental import pallas as pl
from jax.experimental.pallas import tpu as pltpu
from jax.sharding import PartitionSpec as P

NCP = 40000
NOWN = 8192
WIDE = 256
OWN_HIGH = NOWN // WIDE
FEATURES = 64
RIDGE = 4.0
RADIUS = (168.0 / (4.18879 * NCP)) ** (1.0 / 3.0)
F32, BF16, I32 = jnp.float32, jnp.bfloat16, jnp.int32
EXACT = lax.Precision.HIGHEST
NT = (((1,), (1,)), ((), ()))
NN = (((1,), (0,)), ((), ()))


def up_to(value, step):
    return -(-value // step) * step


def rows_iota(shape):
    return lax.broadcasted_iota(I32, shape, 0)


def rounded(value):
    return value.astype(BF16).astype(F32)


def one_hot(index, count):
    return jnp.where(rows_iota((count, index.shape[1])) == index, 1.0, 0.0)


def spread(rows, index_high, count):
    hit = rows_iota((count, index_high.shape[1])) == index_high
    return [jnp.where(hit, row, 0.0) for row in rows]


def stacked_rows(rows):
    sub = rows_iota((8, rows[0].shape[1]))
    tile = jnp.zeros((8, rows[0].shape[1]), F32)
    for number, row in enumerate(rows):
        tile = jnp.where(sub == number, row, tile)
    return tile


def split_features(tile, left):
    sub = rows_iota(tile.shape)
    x = jnp.where(sub < 3, tile, 0.0)
    x1 = rounded(x)
    rest = x - x1
    x2 = rounded(rest)
    x3 = rest - x2
    norm = jnp.sum(x * x, axis=0, keepdims=True)
    n1 = rounded(norm)
    n2 = rounded(norm - n1)
    n3 = norm - n1 - n2
    if left:
        ends = jnp.where(sub == 3, n1, jnp.where(sub == 4, n2, jnp.where(sub == 5, n3, jnp.where(sub < 3, 1.0, 0.0))))
        parts = [-2.0 * part for part in (x1, x2, x1, x2, x3, x1)]
    else:
        ends = jnp.where(sub == 0, n1, jnp.where(sub == 1, n2, jnp.where(sub == 2, n3, jnp.where(sub < 6, 1.0, 0.0))))
        parts = [x1, x1, x2, x2, x1, x3]
    return jnp.concatenate(parts + [ends, jnp.zeros_like(ends)], axis=0)


def wendland_product(weights, left, right):
    squared = lax.dot_general(left, right, NN, preferred_element_type=F32)
    squared = jnp.maximum(squared, 1e-12)
    remaining = jnp.maximum(1.0 - squared * lax.rsqrt(squared), 0.0)
    second = remaining * remaining
    phi = second * second * (1.25 - remaining)
    high = phi.astype(BF16)
    low = (phi - high.astype(F32)).astype(BF16)
    return lax.dot_general(weights, high, NN, preferred_element_type=F32) + lax.dot_general(
        weights, low, NN, preferred_element_type=F32
    )


def split_weights(tile):
    sub = rows_iota(tile.shape)
    head = rounded(tile)
    return jnp.where(sub < 3, head, jnp.where(sub < 6, tile - head, 0.0)).astype(BF16)


def element_kernel(
    adjoint_ref, state_ref, interp_ref, flux_ref, metric_ref, geometry_ref, connect_ref, source_ref,
    nodal_ref, outgoing_ref, adjoint_quad, state_quad, metric_turned, weighted, values, nodes, sums,
    *, halo_high,
):
    basis, quad = interp_ref.shape
    elements, wide = adjoint_ref.shape
    variables = wide // basis
    directions, _, elem_nodes = geometry_ref.shape
    interp = interp_ref[...].astype(F32)
    none = jnp.zeros_like(interp)
    pair = jnp.concatenate([jnp.concatenate([interp, none], axis=1), jnp.concatenate([none, interp], axis=1)], axis=0)
    pair = pair.T.astype(BF16)
    for source, target in ((adjoint_ref, adjoint_quad), (state_ref, state_quad)):
        for couple in range(variables // 2):
            target[couple * 2 * quad : (couple + 1) * 2 * quad, :] = lax.dot_general(
                pair, source[:, couple * 2 * basis : (couple + 1) * 2 * basis], NT, preferred_element_type=F32
            )
    metric_turned[...] = metric_ref[...].T
    nodes[...] = connect_ref[...].T

    def couple_rows(step, carry):
        start = pl.multiple_of(step * 8, 8)
        held = [state_quad[pl.ds(pl.multiple_of(w * quad + start, 8), 8), :] for w in range(variables)]
        metric = metric_turned[pl.ds(start, 8), :]
        for c in range(directions):
            total = None
            for v in range(variables):
                inner = flux_ref[c, v, 0] * held[0]
                for w in range(1, variables):
                    inner = inner + flux_ref[c, v, w] * held[w]
                term = adjoint_quad[pl.ds(pl.multiple_of(v * quad + start, 8), 8), :] * inner
                total = term if total is None else total + term
            weighted[c, pl.ds(start, 8), :] = total * metric
        return carry

    lax.fori_loop(0, quad // 8, couple_rows, 0)
    for c in range(directions):
        partial = lax.dot_general(geometry_ref[c].T, weighted[c], NN, precision=EXACT, preferred_element_type=F32)
        head = rounded(partial)
        values[2 * c] = head
        values[2 * c + 1] = partial - head
    sums[...] = jnp.zeros_like(sums)
    halo_rows = up_to(8 * halo_high, 16)

    def scatter_node(step, carry):
        total = None
        for part in range(2):
            row = step * 2 + part
            node = nodes[pl.ds(row, 1), :]
            low, high = node & (WIDE - 1), lax.shift_right_logical(node, 8)
            terms = [values[k, pl.ds(row, 1), :] for k in range(2 * directions)]
            pieces = spread(terms, high, OWN_HIGH)
            tile = stacked_rows(terms)
            for h in range(halo_rows // 8):
                pieces.append(jnp.where(high == OWN_HIGH + h, tile, 0.0))
            placed = jnp.concatenate(pieces, axis=0).astype(BF16)
            product = lax.dot_general(placed, one_hot(low, WIDE).astype(BF16), NT, preferred_element_type=F32)
            total = product if total is None else total + product
        sums[...] += total
        return carry

    lax.fori_loop(0, elem_nodes // 2, scatter_node, 0)
    for c in range(directions):
        first = 2 * c * OWN_HIGH
        nodal_ref[c] = sums[first : first + OWN_HIGH, :] + sums[first + OWN_HIGH : first + 2 * OWN_HIGH, :]
    base = 2 * directions * OWN_HIGH
    slots = source_ref.shape[1]
    outgoing_ref[...] = jnp.zeros_like(outgoing_ref)
    for peer in range(source_ref.shape[0]):
        source = source_ref[peer : peer + 1, :]
        low, high = source & (WIDE - 1), lax.shift_right_logical(source, 8)
        picked = None
        for h in range(halo_high):
            hot = jnp.where(high == h, one_hot(low, WIDE), 0.0)
            product = lax.dot_general(
                sums[base + 8 * h : base + 8 * h + 8, :], hot, NN, precision=EXACT, preferred_element_type=F32
            )
            picked = product if picked is None else picked + product
        for c in range(directions):
            outgoing_ref[peer, c : c + 1, 0:slots] = picked[2 * c : 2 * c + 1] + picked[2 * c + 1 : 2 * c + 2]


def points_kernel(coords_ref, slot_ref, tiles_ref, surface_ref, table, *, groups, members, share):
    count = groups * members
    block = tiles_ref.shape[1] // count
    group_rows = coords_ref.shape[1] // groups
    tiles_ref[...] = jnp.full_like(tiles_ref, 1e3)
    for k in range(count):
        start = (k // members) * group_rows + (k % members) * share
        length = min(share, group_rows - (k % members) * share)
        if length > 0:
            tiles_ref[0:3, k * block : k * block + length] = (coords_ref[:, start : start + length] - 0.5) * (1.0 / RADIUS)
    highs = count * block // WIDE
    for h in range(highs):
        for c in range(3):
            table[c, h : h + 1, :] = tiles_ref[c : c + 1, h * WIDE : (h + 1) * WIDE]
    slot = slot_ref[...]
    low, high = slot & (WIDE - 1), lax.shift_right_logical(slot, 8)
    hot = one_hot(low, WIDE)
    place = one_hot(high, highs)
    rows = []
    for c in range(3):
        chosen = lax.dot_general(table[c], hot, NN, precision=EXACT, preferred_element_type=F32)
        rows.append(jnp.sum(chosen * place, axis=0, keepdims=True))
    surface_ref[...] = stacked_rows(rows)


def own_kernel(incoming_ref, target_ref, nodal_ref, node_ref, slot_ref, surface_ref, owned_ref, payload_ref):
    directions = nodal_ref.shape[0]
    slots = target_ref.shape[1]
    total = None
    for peer in range(target_ref.shape[0]):
        target = target_ref[peer : peer + 1, :]
        low, high = target & (WIDE - 1), lax.shift_right_logical(target, 8)
        terms = []
        for c in range(directions):
            value = incoming_ref[peer, c : c + 1, 0:slots]
            head = rounded(value)
            terms += [head, value - head]
        placed = jnp.concatenate(spread(terms, high, OWN_HIGH), axis=0).astype(BF16)
        product = lax.dot_general(placed, one_hot(low, WIDE).astype(BF16), NT, preferred_element_type=F32)
        total = product if total is None else total + product
    node = node_ref[...]
    low, high = node & (WIDE - 1), lax.shift_right_logical(node, 8)
    hot = one_hot(low, WIDE)
    place = one_hot(high, OWN_HIGH)
    rows = []
    for c in range(directions):
        first = 2 * c * OWN_HIGH
        owned = nodal_ref[c] + (total[first : first + OWN_HIGH] + total[first + OWN_HIGH : first + 2 * OWN_HIGH])
        for h in range(OWN_HIGH):
            owned_ref[c : c + 1, h * WIDE : (h + 1) * WIDE] = owned[h : h + 1, :]
        chosen = lax.dot_general(owned, hot, NN, precision=EXACT, preferred_element_type=F32)
        rows.append(jnp.sum(chosen * place, axis=0, keepdims=True))
    index = slot_ref[...].astype(F32)
    surface = surface_ref[...]
    tile = stacked_rows([surface[0:1], surface[1:2], surface[2:3]] + rows + [index])
    payload_ref[...] = jnp.broadcast_to(tile[None], payload_ref.shape)


def first_image_kernel(rank_ref, payload_ref, tiles_ref, right_ref, image_ref, sums, own_right, image, left_scratch, weights):
    count, _, surface = payload_ref.shape
    block = right_ref.shape[2]
    highs = count * block // WIDE
    together = 4
    rank = rank_ref[0]
    sums[...] = jnp.zeros_like(sums)

    def gather_rows(step, carry):
        tiles = [payload_ref[step * together + part] for part in range(together)]
        tile = jnp.concatenate(tiles, axis=1)
        slot = tile[6:7].astype(I32)
        low, high = slot & (WIDE - 1), lax.shift_right_logical(slot, 8)
        terms = []
        for c in range(3):
            head = rounded(tile[3 + c : 4 + c])
            terms += [head, tile[3 + c : 4 + c] - head]
        placed = jnp.concatenate(spread(terms, high, highs), axis=0).astype(BF16)
        sums[...] += lax.dot_general(placed, one_hot(low, WIDE).astype(BF16), NT, preferred_element_type=F32)
        left_scratch[pl.ds(pl.multiple_of(step * together * surface, 128), together * surface), :] = split_features(
            tile, True
        ).T.astype(BF16)
        doubled = stacked_rows([tile[3 + c : 4 + c] for c in range(3)] * 2)
        weights[:, pl.ds(pl.multiple_of(step * together * surface, 128), together * surface)] = split_weights(doubled)
        return carry

    lax.fori_loop(0, count // together, gather_rows, 0)
    per = block // WIDE
    for h in range(highs):
        for c in range(3):
            first = 2 * c * highs + h
            right_ref[h // per, c : c + 1, (h % per) * WIDE : (h % per + 1) * WIDE] = (
                sums[first : first + 1, :] + sums[first + highs : first + highs + 1, :]
            )
    own_right[...] = right_ref[rank]
    for j in range(per):
        start = pl.multiple_of(rank * block + j * WIDE, WIDE)
        right = split_features(tiles_ref[:, pl.ds(start, WIDE)], False).astype(BF16)

        def accumulate(step, total):
            begin = pl.multiple_of(step * WIDE, WIDE)
            return total + wendland_product(weights[:, pl.ds(begin, WIDE)], left_scratch[pl.ds(begin, WIDE), :], right)

        total = lax.fori_loop(0, count * surface // WIDE, accumulate, jnp.zeros((8, WIDE), F32))
        lanes = slice(j * WIDE, (j + 1) * WIDE)
        for c in range(3):
            image[c : c + 1, lanes] = 4.0 * (total[c : c + 1] + total[3 + c : 4 + c]) + RIDGE * own_right[c : c + 1, lanes]
    image_ref[...] = jnp.broadcast_to(image[...][None], image_ref.shape)


def curvature_kernel(rank_ref, right_ref, image_ref, tiles_ref, direction_ref, scalars_ref, curve_ref, doubled, left_scratch, weights):
    count, _, block = right_ref.shape
    rank = rank_ref[0]

    def total_of(values):
        return jnp.sum(jnp.sum(values, axis=0), axis=1, keepdims=True)

    right, image = right_ref[...], image_ref[...]
    norm = total_of(right * right)
    step_size = norm / total_of(right * image)
    residual = right - step_size[None] * image
    norm_next = total_of(residual * residual)
    direction = residual + (norm_next / norm)[None] * right
    direction_ref[...] = direction
    doubled[...] = jnp.zeros_like(doubled)
    doubled[:, 0:3, :] = direction
    doubled[:, 3:6, :] = direction
    scalars_ref[...] = jnp.zeros_like(scalars_ref)
    scalars_ref[0:3, :] = jnp.broadcast_to(step_size, (3, 128))
    scalars_ref[3:6, :] = jnp.broadcast_to(norm_next, (3, 128))
    per = block // WIDE
    own = doubled[rank]
    weights[...] = split_weights(own)
    for i in range(per):
        start = pl.multiple_of(rank * block + i * WIDE, WIDE)
        left_scratch[i * WIDE : (i + 1) * WIDE, :] = split_features(tiles_ref[:, pl.ds(start, WIDE)], True).T.astype(BF16)
    half = count // 2

    def columns(step, total):
        offset = step // per
        lane = pl.multiple_of((step - offset * per) * WIDE, WIDE)
        owner = lax.rem(rank + offset, count)
        right = split_features(tiles_ref[:, pl.ds(pl.multiple_of(owner * block + lane, WIDE), WIDE)], False).astype(BF16)
        product = None
        for i in range(per):
            term = wendland_product(weights[:, i * WIDE : (i + 1) * WIDE], left_scratch[i * WIDE : (i + 1) * WIDE, :], right)
            product = term if product is None else product + term
        factor = jnp.where((offset == 0) | (offset == half), 1.0, 2.0)
        return total + factor * (product * doubled[owner, :, pl.ds(lane, WIDE)])

    total = lax.fori_loop(0, (half + 1) * per, columns, jnp.zeros((8, WIDE), F32))
    sub = rows_iota(own.shape)
    ridge = RIDGE * jnp.sum(jnp.where(sub < 3, own * own, 0.0), axis=1, keepdims=True)
    curve = 4.0 * jnp.sum(total, axis=1, keepdims=True) + ridge
    curve_ref[...] = jnp.broadcast_to(curve[None], curve_ref.shape)


def finish_kernel(rank_ref, curve_ref, scalars_ref, right_ref, direction_ref, point_ref, *, members, share):
    curve = jnp.sum(curve_ref[...], axis=0)
    curve = curve[0:3] + curve[3:6]
    step_size = scalars_ref[0:3, 0:1]
    second = scalars_ref[3:6, 0:1] / curve[:, 0:1]
    first_block = (rank_ref[0] // members) * members
    total = point_ref.shape[1]
    for member in range(members):
        length = min(share, total - member * share)
        if length > 0:
            value = step_size * right_ref[first_block + member] + second * direction_ref[first_block + member]
            point_ref[:, member * share : member * share + length] = value[:, 0:length]


def call(body, outs, scratch, scalars=(), **cost):
    def run(*operands):
        specs = [
            pl.BlockSpec(memory_space=pltpu.SMEM if number in scalars else pltpu.VMEM) for number in range(len(operands))
        ]
        return pl.pallas_call(
            body,
            out_shape=[jax.ShapeDtypeStruct(shape, F32) for shape in outs],
            in_specs=specs,
            out_specs=[pl.BlockSpec(memory_space=pltpu.VMEM)] * len(outs),
            scratch_shapes=[pltpu.VMEM(shape, kind) for shape, kind in scratch],
            compiler_params=pltpu.CompilerParams(vmem_limit_bytes=48 << 20),
            cost_estimate=pl.CostEstimate(transcendentals=0, **cost),
        )(*operands)

    return run


def on_device(
    adjoint, state, interp, flux_weights, metric, geometry, connectivity, halo_source, halo_target,
    surface_node, surface_point, point_coords,
):
    members, groups = lax.axis_size("dev"), lax.axis_size("grp")
    count = members * groups
    both = ("grp", "dev")
    rank = (lax.axis_index("grp") * members + lax.axis_index("dev")).astype(I32).reshape(1)
    halo_count = halo_source.shape[1] * (members - 1) // 2
    halo_high = halo_count // WIDE + 1
    elements = adjoint.shape[0]
    basis, quad = interp.shape
    wide = adjoint.shape[1] // basis * quad
    elem_nodes = geometry.shape[2]
    surface = surface_node.shape[0]
    group_rows = NCP // groups
    share = -(-group_rows // members)
    block = up_to(share, WIDE)
    highs = count * block // WIDE
    in_group = surface_point % group_rows
    slot = (surface_point // group_rows * members + in_group // share) * block + in_group % share
    slot = slot.reshape(1, surface)
    node = surface_node.reshape(1, surface)
    halo_rows = up_to(8 * halo_high, 16)

    nodal, outgoing = call(
        functools.partial(element_kernel, halo_high=halo_high),
        [(3, OWN_HIGH, WIDE), (members, 8, 128)],
        [
            ((wide, elements), F32), ((wide, elements), F32), ((quad, elements), F32), ((3, quad, elements), F32),
            ((6, elem_nodes, elements), F32), ((elem_nodes, elements), I32), ((6 * OWN_HIGH + halo_rows, WIDE), F32),
        ],
        scalars=(3,), flops=10**10, bytes_accessed=2 * 10**6,
    )(adjoint, state, interp, flux_weights, metric, geometry, connectivity, halo_source)
    incoming = lax.all_to_all(outgoing, "dev", split_axis=0, concat_axis=0, tiled=True)
    tiles, surface_tile = call(
        functools.partial(points_kernel, groups=groups, members=members, share=share),
        [(8, count * block), (8, surface)],
        [((3, highs, WIDE), F32)],
        flops=10**9, bytes_accessed=2 * 10**6,
    )(point_coords, slot)
    owned, payload = call(
        own_kernel, [(3, NOWN), (count, 8, surface)], [], flops=10**9, bytes_accessed=10**6
    )(incoming, halo_target, nodal, node, slot, surface_tile)
    payload = lax.all_to_all(payload, both, split_axis=0, concat_axis=0, tiled=True)
    right_side, image = call(
        first_image_kernel,
        [(count, 3, block), (count, 3, block)],
        [
            ((6 * highs, WIDE), F32), ((3, block), F32), ((3, block), F32),
            ((count * surface, FEATURES), BF16), ((8, count * surface), BF16),
        ],
        scalars=(0,), flops=10**10, bytes_accessed=4 * 10**6,
    )(rank, payload, tiles)
    image = lax.all_to_all(image, both, split_axis=0, concat_axis=0, tiled=True)
    direction, scalars, curve = call(
        curvature_kernel,
        [(count, 3, block), (8, 128), (count, 8, 1)],
        [((count, 8, block), F32), ((block, FEATURES), BF16), ((8, block), BF16)],
        scalars=(0,), flops=5 * 10**10, bytes_accessed=4 * 10**6,
    )(rank, right_side, image, tiles)
    curve = lax.all_to_all(curve, both, split_axis=0, concat_axis=0, tiled=True)
    (solution_rows,) = call(
        functools.partial(finish_kernel, members=members, share=share),
        [(3, group_rows)], [], scalars=(0,), flops=10**6, bytes_accessed=2 * 10**6,
    )(rank, curve, scalars, right_side, direction)
    return (owned, solution_rows)


def solution(mesh):
    shard = P(("grp", "dev"), None)
    line = P(("grp", "dev"))
    return jax.shard_map(
        on_device,
        mesh=mesh,
        in_specs=(shard, shard, P(), P(), shard, P(), shard, shard, shard, line, line, P()),
        out_specs=(P(None, ("grp", "dev")), P(None, "grp")),
        check_vma=False,
    )
```
